32 devices in a mesh: groups: 2 (over y), seq: 4 (over z), query: 2 (over x), chan: 2 (over core).
Axes of the slice: x: 2, y: 2, z: 4, core: 2. Of those that a mesh axis runs over, the one named last changes fastest.
Arguments:
- hidden_rows: bfloat16 [4, 1024, 4096], P(('groups', 'query'), 'seq', 'chan'), parts along dimension 0, may hold values from -6 to 6
- scan_grad: bfloat16 [4, 1024, 8192], P(('groups', 'query'), 'seq', 'chan'), parts along dimension 0, may hold values from -6 to 6
- step_size: bfloat16 [4, 1024, 8192], P(('groups', 'query'), 'seq', 'chan'), parts along dimension 0, as said below
- state_proj: bfloat16 [4, 2, 16, 1024], P(('groups', 'query'), None, None, 'seq'), parts along dimension 0, may hold values from -6 to 6
- decay_rate: float32 [16, 8192], P(None, 'chan'), as said below
- skip_gain: float32 [8192], P('chan'), may hold values from 0.5 to 1.5
- in_sketch: bfloat16 [4096, 64], P('chan'), may hold values from -0.09375 to 0.09375
- out_sketch: bfloat16 [8192, 64], P('chan'), may hold values from -0.0625 to 0.0625
- doc_lengths: int32 [4, 8], P(('groups', 'query')), parts along dimension 0, may hold values from 1 to 512, 1024 in all within a row
- doc_slot: int32 [4, 8], P(('groups', 'query')), parts along dimension 0, may hold values from 0 to 7, each once within a row
- query_sketch: bfloat16 [32, 4096], P(('query', 'chan')), may hold values from -0.09375 to 0.09375
Outputs:
- scores: float32 [4, 8, 32], P(('groups', 'query'), 'seq'), parts along dimension 0
The draws below stay inside these ranges and needn't reach their ends.
There are 2 independent parts, one for each index of `groups`. The reference program is written for one: setup_inputs(seed, part) draws one part's arguments, and reference() takes and returns one part's arrays. A program takes and returns all parts, laid end to end along the dimension named above; an argument that names none is the same for every part. Nothing has to cross between parts.
Inputs may be any that keep to these rules, and one draw needn't show every extreme that they name: `doc_lengths`: each row lists one sequence's documents in order; the lengths of a row sum to 1024 and the longest is exactly 512. `doc_slot`: each row names every slot once; slot k belongs to seq index k // 2. `step_size`: positive. `decay_rate`: positive.
All inputs are finite; a program needn't handle non-finite values.
Results may differ from the reference program's by a relative error of at most 0.0057.
Values may be sent and summed in bfloat16 or wider, within the bound.
A program may use at most 64 MiB of HBM per device.

```python
import math
import jax
import jax.numpy as jnp
import numpy as np
from jax import lax

D = 4096
INNER = 8192
NSTATE = 16
SK = 64
SPAN_WIDTH = 1024
DOCS = 8
SEQS = 2
QUERIES = 32


def draw_step_size(key, part):
    key = jax.random.fold_in(key, 23)
    base_key, spot_key, lift_key = jax.random.split(key, 3)
    unit = jax.random.uniform(base_key, (SEQS, SPAN_WIDTH, INNER), jnp.float32)
    starting_shift = 0.5 * jnp.exp(unit * jnp.log(4.0))
    chosen_places = jax.random.randint(spot_key, (SEQS, 4), 0, SPAN_WIDTH)
    cluster_items = jnp.any(jnp.arange(SPAN_WIDTH)[None, :, None] == chosen_places[:, None, :], axis=-1)
    raising_scalar = jax.random.uniform(lift_key, (SEQS, SPAN_WIDTH, 1), jnp.float32, 8.0, 24.0)
    return jnp.where(cluster_items[:, :, None], starting_shift * raising_scalar, starting_shift).astype(jnp.bfloat16)


def draw_decay_rate(key, part):
    key = jax.random.fold_in(key, 11)
    unit = jax.random.uniform(key, (NSTATE, INNER), jnp.float32)
    lowest = 0.02 / SPAN_WIDTH
    highest = 0.03
    return lowest * jnp.exp(unit * jnp.log(highest / lowest))


def level_of(own_key, dims, cuts, low, high):
    factor_of, own = 1.0, jax.random.fold_in(own_key, 6)
    for position, parts in cuts:
        heights = jnp.exp(jax.random.uniform(jax.random.fold_in(own, position), (parts,), jnp.float32, low / len(cuts), high / len(cuts)))
        factor_of = factor_of * jnp.repeat(heights, dims[position] // parts).reshape([-1 if axis == position else 1 for axis in range(len(dims))])
    return factor_of


def length_profile(amount, total, reach, skew):
    portions = [(1 << 20) // math.isqrt(grade ** skew) + 1 for grade in range(2, amount + 1)]
    rest, counts = total - reach - (amount - 1), [1] * (amount - 1)
    while rest > 0:
        free = [i for i in range(amount - 1) if counts[i] < reach]
        mass, left = sum([portions[i] for i in free]), rest
        for i in free:
            more = min(reach - counts[i], max(1, left * portions[i] // mass), rest)
            counts[i] = counts[i] + more
            rest = rest - more
    return np.array([reach] + counts)


def uneven(own_key, count, total, bound, skew):
    if count == 2:
        one = jax.random.randint(own_key, (), max(1, total - bound), min(bound, total - 1) + 1)
        return jnp.stack([one, total - one])
    lengths = jnp.asarray(length_profile(count, total, bound, skew), jnp.int32)
    twos = (count - 1) // 2
    giver, taker = lengths[1:1 + 2 * twos:2], lengths[2:2 + 2 * twos:2]
    margin = jnp.minimum(giver - 1, bound - taker)
    passed = jax.random.randint(jax.random.fold_in(own_key, 1), (twos,), 0, 1 << 20) % (margin + 1)
    lengths = lengths.at[1:1 + 2 * twos:2].set(giver - passed).at[2:2 + 2 * twos:2].set(taker + passed)
    return lengths[jax.random.permutation(jax.random.fold_in(own_key, 2), count)]


def scatter_about(key, dims, deviation, bound, cuts=(), kind=jnp.bfloat16):
    drawn = deviation * jax.random.normal(key, dims, jnp.float32)
    if cuts:
        drawn = drawn * level_of(key, dims, cuts, -0.22, 0.18)
    return jnp.clip(drawn, -bound, bound).astype(kind)


def setup_inputs(seed: int = 0, part: int = 0) -> dict:
    keys = jax.random.split(jax.random.key(seed), 12)
    part_splits = jax.random.split(jax.random.fold_in(keys[11], part), 12)
    return {
        "hidden_rows": scatter_about(part_splits[0], (SEQS, SPAN_WIDTH, D), 1.0, 6.0, ((0, 2), (1, 4), (2, 2))),
        "scan_grad": scatter_about(part_splits[1], (SEQS, SPAN_WIDTH, INNER), 1.0, 6.0, ((0, 2), (1, 4), (2, 2))),
        "step_size": draw_step_size(jax.random.fold_in(jax.random.fold_in(keys[11], part), 71), part),
        "state_proj": scatter_about(part_splits[3], (SEQS, 2, NSTATE, SPAN_WIDTH), 1.0, 6.0, ((0, 2), (3, 4))),
        "decay_rate": draw_decay_rate(jax.random.fold_in(keys[11], 71), part),
        "skip_gain": jnp.clip(0.5 + 1.0 * jax.random.uniform(keys[5], (INNER,), jnp.float32) ** level_of(keys[5], (INNER,), ((0, 2),), -0.2, 0.2), 0.5, 1.5),
        "in_sketch": scatter_about(keys[6], (D, SK), D ** -0.5, 0.09375, ((0, 2),)),
        "out_sketch": scatter_about(keys[7], (INNER, SK), INNER ** -0.5, 0.0625, ((0, 2),)),
        "doc_lengths": jax.vmap(lambda own: uneven(own, DOCS, SPAN_WIDTH, SPAN_WIDTH // 2, 2))(jax.random.split(part_splits[8], SEQS)).reshape((SEQS, DOCS)).astype(jnp.int32),
        "doc_slot": jax.vmap(lambda own: jax.random.permutation(own, DOCS))(jax.random.split(part_splits[9], SEQS)).reshape((SEQS, DOCS)).astype(jnp.int32),
        "query_sketch": scatter_about(keys[10], (QUERIES, SK * SK), (SK * SK) ** -0.5, 0.09375, ((0, 4),)),
    }


def adjoint_scan(grad_rows, step_rows, in_rows, out_rows, retain_mask, decay_rate, skip_gain):

    def one_token(state_now, inputs):
        grad_now, step_now, in_now, out_now, keep_now = inputs
        grad_f = grad_now.astype(jnp.float32)
        step_f = step_now.astype(jnp.float32)
        adjoint = out_now.astype(jnp.float32)[:, None] * grad_f[None, :] + state_now
        input_grad = skip_gain * grad_f + step_f * lax.optimization_barrier(jnp.sum(in_now.astype(jnp.float32)[:, None] * adjoint, axis=0))
        state_now = jnp.exp(-step_f[None, :] * decay_rate) * keep_now * adjoint
        return (state_now, input_grad.astype(jnp.bfloat16))
    start_state = jnp.zeros((NSTATE, INNER), jnp.float32)
    _, input_grads = lax.scan(one_token, start_state, (grad_rows, step_rows, in_rows, out_rows, retain_mask), reverse=True)
    return input_grads

def sequence_scores(hidden_seq, grad_seq, step_seq, proj_seq, decay_rate, skip_gain, in_sketch, out_sketch, lengths_row, slots_row, query_sketch):
    doc_ends = jnp.cumsum(lengths_row).astype(jnp.int32)
    doc_starts = doc_ends - lengths_row
    positions = jnp.arange(SPAN_WIDTH, dtype=jnp.int32)
    member_index = (positions[:, None] >= doc_starts[None, :]) & (positions[:, None] < doc_ends[None, :])
    retain_mask = 1.0 - jnp.any(positions[:, None] == doc_starts[None, :], axis=1).astype(jnp.float32)
    input_grads = adjoint_scan(grad_seq, step_seq, proj_seq[0].T, proj_seq[1].T, retain_mask, decay_rate, skip_gain)
    entry_facet = jnp.dot(hidden_seq, in_sketch, preferred_element_type=jnp.float32).astype(jnp.bfloat16)
    out_side = jnp.dot(input_grads, out_sketch, preferred_element_type=jnp.float32).astype(jnp.bfloat16)
    weighted = (member_index.astype(jnp.bfloat16)[:, :, None] * out_side[:, None, :]).reshape(SPAN_WIDTH, DOCS * SK)
    sketch = jnp.einsum('tk,tj->kj', weighted.astype(jnp.float32), entry_facet.astype(jnp.float32)).reshape(DOCS, SK * SK)
    slotted = jnp.zeros_like(sketch).at[slots_row].set(sketch)
    mean_square = lax.optimization_barrier(jnp.mean(slotted * slotted, axis=1, keepdims=True))
    normed = (slotted * lax.rsqrt(mean_square + 1e-06)).astype(jnp.bfloat16)
    return jnp.dot(normed, query_sketch.T, preferred_element_type=jnp.float32)

def reference(hidden_rows, scan_grad, step_size, state_proj, decay_rate, skip_gain, in_sketch, out_sketch, doc_lengths, doc_slot, query_sketch):
    results = []
    for seq_number in range(SEQS):
        results.append(sequence_scores(hidden_rows[seq_number], scan_grad[seq_number], step_size[seq_number], state_proj[seq_number], decay_rate, skip_gain, in_sketch, out_sketch, doc_lengths[seq_number], doc_slot[seq_number], query_sketch))
    return jnp.stack(results)
```

```python
import math

import jax
import jax.numpy as jnp
from jax import lax
from jax.experimental import pallas as pl
from jax.experimental.pallas import tpu as pltpu
from jax.sharding import PartitionSpec as P

SLOT = 2
epsilon = 1e-06
LANES = 128
GROUP = 16
CHUNK = 1024
TINY = 1.1754944e-38


def lane_tiles(width):
    return [slice(t * LANES, (t + 1) * LANES) for t in range(width // LANES)]


def scan_kernel(grad, step, rate, out_table, in_diag, reset, y, carry_out, step_f, grad_f, states):
    rows, width = grad.shape
    count = rate.shape[0]
    tiles = lane_tiles(width)
    step_f[...] = step[...].astype(jnp.float32) + reset[...]
    grad_f[...] = grad[...].astype(jnp.float32)
    rates = [rate[:, t] for t in tiles]

    def one_group(index, carry):
        group = rows // GROUP - 1 - index
        first = pl.multiple_of(group * GROUP, GROUP)
        near_step = step_f.at[pl.ds(first, GROUP), :]
        near_grad = grad_f.at[pl.ds(first, GROUP), :]
        for offset in reversed(range(GROUP)):
            row = first + offset
            weight = out_table[pl.ds(pl.multiple_of(row * count, count), count), :]
            fresh = []
            for t, a, held in zip(tiles, rates, carry):
                adjoint = weight * near_grad[offset : offset + 1, t] + held
                states[offset * count : (offset + 1) * count, t] = adjoint.astype(jnp.bfloat16)
                fresh.append(jnp.exp2(near_step[offset : offset + 1, t] * a) * adjoint)
            carry = fresh
        y[pl.ds(first, GROUP), :] = jnp.dot(
            in_diag[pl.ds(first, GROUP), :], states[...], preferred_element_type=jnp.float32
        )
        return carry

    start = [jnp.zeros((count, LANES), jnp.float32) for _ in tiles]
    last = lax.fori_loop(0, rows // GROUP, one_group, start)
    for t, value in zip(tiles, last):
        carry_out[:, t] = value


def join_kernel(
    grad, step, rate, in_diag, later, skip, y, incoming, sketch, side, suffix, states, mixed
):
    rows, width = grad.shape
    count = rate.shape[0]
    tiles = lane_tiles(width)
    suffix[...] = jnp.dot(later[...], step[...], preferred_element_type=jnp.float32)
    rates = [rate[:, t] for t in tiles]
    enters = [incoming[:, t] for t in tiles]

    def one_group(group, _):
        first = pl.multiple_of(group * GROUP, GROUP)
        near = suffix.at[pl.ds(first, GROUP), :]
        for offset in range(GROUP):
            one = slice(offset, offset + 1)
            for t, a, e in zip(tiles, rates, enters):
                value = jnp.exp2(near[one, t] * a) * e
                states[offset * count : (offset + 1) * count, t] = value.astype(jnp.bfloat16)
        added = jnp.dot(
            in_diag[pl.ds(first, GROUP), :], states[...], preferred_element_type=jnp.float32
        )
        here = pl.ds(first, GROUP)
        total = y[here, :] + added
        result = skip[...] * grad[here, :].astype(jnp.float32) + step[here, :].astype(
            jnp.float32
        ) * total
        mixed[here, :] = result.astype(jnp.bfloat16)
        return 0

    lax.fori_loop(0, rows // GROUP, one_group, 0)
    part = jnp.dot(mixed[...], sketch[...], preferred_element_type=jnp.float32)

    @pl.when(pl.program_id(0) == 0)
    def _():
        side[...] = part

    @pl.when(pl.program_id(0) > 0)
    def _():
        side[...] += part


def whole(shape):
    return pl.BlockSpec(shape, lambda i: (0,) * len(shape))


def columns(height, width):
    return pl.BlockSpec((height, width), lambda i: (0, i))


def run_scan(grad, step, rate, out_table, in_diag, reset):
    rows, channels = grad.shape
    count = rate.shape[0]
    return pl.pallas_call(
        scan_kernel,
        grid=(channels // CHUNK,),
        in_specs=[
            columns(rows, CHUNK),
            columns(rows, CHUNK),
            columns(count, CHUNK),
            whole(out_table.shape),
            whole(in_diag.shape),
            whole(reset.shape),
        ],
        out_specs=[columns(rows, CHUNK), columns(count, CHUNK)],
        out_shape=[
            jax.ShapeDtypeStruct((rows, channels), jnp.float32),
            jax.ShapeDtypeStruct((count, channels), jnp.float32),
        ],
        scratch_shapes=[
            pltpu.VMEM((rows, CHUNK), jnp.float32),
            pltpu.VMEM((rows, CHUNK), jnp.float32),
            pltpu.VMEM((GROUP * count, CHUNK), jnp.bfloat16),
        ],
        compiler_params=pltpu.CompilerParams(vmem_limit_bytes=48 * 2**20),
        name="scan",
    )(grad, step, rate, out_table, in_diag, reset)


def run_join(grad, step, rate, in_diag, later, skip, y, incoming, sketch):
    rows, channels = grad.shape
    count = rate.shape[0]
    return pl.pallas_call(
        join_kernel,
        grid=(channels // CHUNK,),
        in_specs=[
            columns(rows, CHUNK),
            columns(rows, CHUNK),
            columns(count, CHUNK),
            whole(in_diag.shape),
            whole(later.shape),
            columns(1, CHUNK),
            columns(rows, CHUNK),
            columns(count, CHUNK),
            pl.BlockSpec((CHUNK, sketch.shape[1]), lambda i: (i, 0)),
        ],
        out_specs=whole((rows, sketch.shape[1])),
        out_shape=jax.ShapeDtypeStruct((rows, sketch.shape[1]), jnp.float32),
        scratch_shapes=[
            pltpu.VMEM((rows, CHUNK), jnp.float32),
            pltpu.VMEM((GROUP * count, CHUNK), jnp.bfloat16),
            pltpu.VMEM((rows, CHUNK), jnp.bfloat16),
        ],
        compiler_params=pltpu.CompilerParams(vmem_limit_bytes=48 * 2**20),
        name="join",
    )(grad, step, rate, in_diag, later, skip, y, incoming, sketch)


def shifted(block, axis, distance):
    devices = range(lax.axis_size(axis))
    route = [(i - distance, i) for i in devices if i - distance in devices]
    return lax.ppermute(block, axis, route)


def doc_sketch(entry_facet, out_side, positions, doc_starts, doc_ends, slot_pick):
    member_index = (
        (positions[:, None] >= doc_starts[None, :]) & (positions[:, None] < doc_ends[None, :])
    ).astype(jnp.float32)
    chosen = jnp.dot(member_index, slot_pick.T).astype(jnp.bfloat16)
    row_count = out_side.shape[0]
    weighted = (chosen[:, :, None] * out_side[:, None, :]).reshape(row_count, -1)
    product_sum = jnp.einsum("tk,tj->kj", weighted, entry_facet, preferred_element_type=jnp.float32)
    return product_sum.reshape(slot_pick.shape[0], -1)


def local(
    hidden_rows,
    scan_grad,
    step_size,
    state_proj,
    decay_rate,
    skip_gain,
    in_sketch,
    out_sketch,
    doc_lengths,
    doc_slot,
    query_sketch,
):
    tok_count = scan_grad.shape[1]
    seq_devices = lax.axis_size("seq")
    seq_index = lax.axis_index("seq")
    positions = seq_index * tok_count + jnp.arange(tok_count, dtype=jnp.int32)
    lengths_row = doc_lengths[0]
    doc_ends = jnp.cumsum(lengths_row)
    doc_starts = doc_ends - lengths_row
    retain_mask = 1.0 - jnp.any(positions[:, None] == doc_starts[None, :], axis=1).astype(
        jnp.float32
    )
    grad_rows = scan_grad[0]
    step_rows = step_size[0]
    count = decay_rate.shape[0]
    rate = -jnp.maximum(decay_rate * math.log2(math.e), TINY)
    reset = jnp.where(retain_mask > 0.0, 0.0, jnp.inf).astype(jnp.float32)[:, None]
    out_table = jnp.broadcast_to(
        state_proj[0, 1].T.astype(jnp.float32)[:, :, None], (tok_count, count, LANES)
    ).reshape(tok_count * count, LANES)
    line = jnp.arange(tok_count, dtype=jnp.int32)
    place = jnp.arange(GROUP * count, dtype=jnp.int32)
    on_line = (line[:, None] % GROUP) == (place[None, :] // count)
    in_wide = jnp.tile(state_proj[0, 0].T, (1, GROUP))
    in_diag = jnp.where(on_line, in_wide, 0).astype(jnp.bfloat16)
    still_open = jnp.flip(jnp.cumprod(jnp.flip(jnp.roll(retain_mask, -1).at[-1].set(1.0))))
    in_open = jnp.where(still_open[:, None] > 0.0, in_diag, 0).astype(jnp.bfloat16)
    later = (line[:, None] < line[None, :]).astype(jnp.bfloat16)
    y, local_end = run_scan(grad_rows, step_rows, rate, out_table, in_diag, reset)
    step_total = jnp.sum(step_rows.astype(jnp.float32), axis=0)
    through = jnp.exp2(rate * step_total[None, :]) * jnp.prod(retain_mask)
    in_side_part = jnp.dot(hidden_rows[0], in_sketch, preferred_element_type=jnp.float32)

    def relay(turn_index, received):
        departing_rows = through * received + local_end
        return shifted(departing_rows, "seq", -1)

    incoming = lax.fori_loop(0, seq_devices - 1, relay, jnp.zeros_like(local_end))
    out_side_part = run_join(
        grad_rows, step_rows, rate, in_open, later, skip_gain[None, :], y, incoming, out_sketch
    )
    entry_facet, out_side = lax.psum((in_side_part, out_side_part), "chan")
    entry_facet = entry_facet.astype(jnp.bfloat16)
    out_side = out_side.astype(jnp.bfloat16)
    slots_row = doc_slot[0]
    document_count = slots_row.shape[0]
    owned_slots = seq_index * SLOT + jnp.arange(SLOT, dtype=jnp.int32)
    own_pick = (slots_row[None, :] == owned_slots[:, None]).astype(jnp.float32)
    every_pick = jnp.eye(document_count, dtype=jnp.float32)
    doc_partial = doc_sketch(entry_facet, out_side, positions, doc_starts, doc_ends, every_pick)
    summed = lax.psum(doc_partial, "seq")
    own_sketch = jnp.dot(own_pick, summed, precision=lax.Precision.HIGHEST)
    mean_square = jnp.mean(own_sketch * own_sketch, axis=1, keepdims=True)
    normed = (own_sketch * lax.rsqrt(mean_square + epsilon)).astype(jnp.bfloat16)
    scores = lax.dot_general(
        normed,
        lax.all_gather(query_sketch, ("query", "chan"), axis=0, tiled=True),
        (((1,), (1,)), ((), ())),
        preferred_element_type=jnp.float32,
    )
    return scores[None]


def solution(mesh):
    placed = (
        P(("groups", "query"), "seq", "chan"),
        P(("groups", "query"), "seq", "chan"),
        P(("groups", "query"), "seq", "chan"),
        P(("groups", "query"), None, None, "seq"),
        P(None, "chan"),
        P("chan"),
        P("chan", None),
        P("chan", None),
        P(("groups", "query"), None),
        P(("groups", "query"), None),
        P(("query", "chan"), None),
    )
    return jax.shard_map(
        local,
        mesh=mesh,
        in_specs=placed,
        out_specs=P(("groups", "query"), "seq", None),
        check_vma=False,
    )
```

```python
import functools
import math

import jax
import jax.numpy as jnp
from jax import lax
from jax.experimental import pallas as pl
from jax.experimental.pallas import tpu as pltpu
from jax.sharding import PartitionSpec as P

EPSILON = 1e-06
LANES = 128
GROUP = 32
FOLD = 8
PACK = 16
CHUNK = 1024
TINY = 1.1754944e-38
F32 = jnp.float32
BF16 = jnp.bfloat16
MESH = pl.DeviceIdType.MESH
LAST = (((1,), (1,)), ((), ()))
FIRST = (((0,), (0,)), ((), ()))


def lane_tiles(width):
    return [slice(t * LANES, (t + 1) * LANES) for t in range(width // LANES)]


def dot(a, b, dims=None, precision=None):
    if dims is None:
        dims = (((1,), (0,)), ((), ()))
    return lax.dot_general(a, b, dims, preferred_element_type=F32, precision=precision)


def kernel(
    seq_total,
    query_total,
    chan_total,
    lengths,
    slots,
    hidden,
    grad,
    step,
    proj,
    decay,
    skip,
    in_sketch,
    out_sketch,
    queries,
    scores,
    step_f,
    grad_f,
    states,
    local_y,
    mixed,
    out_table,
    in_table,
    in_diag,
    open_diag,
    reset,
    member,
    ends,
    inbox,
    outbox,
    in_own,
    in_peer,
    out_own,
    out_peer,
    sketch_part,
    sketch_peer,
    query_all,
    relay_send,
    relay_recv,
    pair_send,
    pair_recv,
    query_send,
    query_recv,
    sketch_send,
    sketch_recv,
):
    rows, channels = grad.shape
    count = decay.shape[0]
    docs = lengths.shape[1]
    owned = docs // seq_total
    side = LANES // owned
    chunks = channels // CHUNK
    tiles = lane_tiles(CHUNK)
    seq = lax.axis_index("seq")
    query = lax.axis_index("query")
    chan = lax.axis_index("chan")
    quarter = query * chan_total + chan
    team = query_total * chan_total

    def seq_peer(offset):
        return {"seq": lax.rem(seq + offset, seq_total)}

    def team_peer(offset):
        other = lax.rem(quarter + offset, team)
        return {"query": lax.div(other, chan_total), "chan": lax.rem(other, chan_total)}

    barrier = pltpu.get_barrier_semaphore()
    for offset in range(1, seq_total):
        pl.semaphore_signal(barrier, inc=1, device_id=seq_peer(offset), device_id_type=MESH)
    for offset in range(1, team):
        pl.semaphore_signal(barrier, inc=1, device_id=team_peer(offset), device_id_type=MESH)
    pl.semaphore_wait(barrier, seq_total + team - 2)

    def query_copy(offset):
        return pltpu.make_async_remote_copy(
            src_ref=queries,
            dst_ref=query_all.at[quarter],
            send_sem=query_send.at[offset - 1],
            recv_sem=query_recv.at[offset - 1],
            device_id=team_peer(offset),
            device_id_type=MESH,
        )

    def pair_copy(source, target, index):
        return pltpu.make_async_remote_copy(
            src_ref=source,
            dst_ref=target,
            send_sem=pair_send.at[index],
            recv_sem=pair_recv.at[index],
            device_id={"chan": 1 - chan},
            device_id_type=MESH,
        )

    def relay_copy(index):
        return pltpu.make_async_remote_copy(
            src_ref=outbox.at[index],
            dst_ref=inbox.at[index],
            send_sem=relay_send.at[index],
            recv_sem=relay_recv.at[index],
            device_id={"seq": lax.rem(seq + seq_total - 1, seq_total)},
            device_id_type=MESH,
        )

    def sketch_copy(offset):
        return pltpu.make_async_remote_copy(
            src_ref=sketch_part.at[lax.rem(seq + offset, seq_total)],
            dst_ref=sketch_peer.at[offset - 1],
            send_sem=sketch_send.at[offset - 1],
            recv_sem=sketch_recv.at[offset - 1],
            device_id=seq_peer(offset),
            device_id_type=MESH,
        )

    for offset in range(1, team):
        query_copy(offset).start()
    in_own[...] = dot(hidden[...], in_sketch[...], LAST)
    pair_copy(in_own, in_peer, 0).start()

    begin = seq * rows
    line = begin + lax.broadcasted_iota(jnp.int32, (rows, LANES), 0)
    lane_slot = lax.broadcasted_iota(jnp.int32, (rows, LANES), 1) // side

    def mark_starts(k, carry):
        start, is_start, is_shut, is_any = carry
        is_start = jnp.where(line == start, 1.0, is_start)
        inside = (start > line) & (start < begin + rows)
        is_shut = jnp.where(inside, 1.0, is_shut)
        first = jnp.full(is_any.shape, start, jnp.int32)
        held = (first >= begin) & (first < begin + rows)
        is_any = jnp.where(held, 1.0, is_any)
        return start + lengths[0, k], is_start, is_shut, is_any

    empty = jnp.zeros((rows, LANES), F32)
    _, is_start, is_shut, is_any = lax.fori_loop(
        0, docs, mark_starts, (jnp.int32(0), empty, empty, jnp.zeros((count, LANES), F32))
    )
    reset[...] = jnp.where(is_start > 0.0, jnp.inf, 0.0)
    keep_all = 1.0 - is_any
    is_open = 1.0 - is_shut

    def owner_mask(owner, _):
        def mark(k, carry):
            start, mask = carry
            stop = start + lengths[0, k]
            hit = (lane_slot + owner * owned == slots[0, k]) & (line >= start) & (line < stop)
            return stop, jnp.where(hit, 1.0, mask)

        _, mask = lax.fori_loop(0, docs, mark, (jnp.int32(0), empty))
        member[owner] = mask.astype(BF16)
        return 0

    lax.fori_loop(0, seq_total, owner_mask, 0)

    wide = (PACK * count, rows)
    row_place = lax.broadcasted_iota(jnp.int32, wide, 0) // count
    row_line = lax.broadcasted_iota(jnp.int32, wide, 1)
    ones = jnp.ones((rows, LANES), BF16)
    spreads = [jnp.concatenate([proj[i].astype(F32)] * PACK, axis=0) for i in range(2)]

    def fill_tables(group, _):
        here = pl.ds(pl.multiple_of(group * PACK * count, PACK * count), PACK * count)
        for table, spread in zip((in_table, out_table), spreads):
            picked = jnp.where(row_line == row_place + group * PACK, spread, 0.0).astype(BF16)
            table[here, :] = dot(picked, ones)
        return 0

    lax.fori_loop(0, rows // PACK, fill_tables, 0)

    deep = (rows, GROUP * FOLD)
    on_line = lax.rem(lax.broadcasted_iota(jnp.int32, deep, 0), GROUP) == (
        lax.broadcasted_iota(jnp.int32, deep, 1) // FOLD
    )
    diag = on_line.astype(F32)
    in_diag[...] = diag.astype(BF16)
    open_wide = jnp.concatenate([is_open] * (GROUP * FOLD // LANES), axis=1)
    open_diag[...] = (diag * open_wide).astype(BF16)

    def folded(value):
        parts = [value[i : i + FOLD] for i in range(0, count, FOLD)]
        return sum(parts[1:], parts[0])

    def rate_of(columns):
        return -jnp.maximum(decay[:, columns] * math.log2(math.e), TINY)

    def chunk_tiles(chunk):
        base = chunk * CHUNK
        return [pl.ds(pl.multiple_of(base + t * LANES, LANES), LANES) for t in range(len(tiles))]

    def relay(chunk):
        @pl.when(seq < seq_total - 1)
        def _():
            relay_copy(chunk).wait_recv()

        @pl.when(seq == seq_total - 1)
        def _():
            inbox[chunk] = jnp.zeros((count, CHUNK), F32)

        @pl.when(seq > 0)
        def _():
            here = pl.ds(pl.multiple_of(chunk * CHUNK, CHUNK), CHUNK)
            total = dot(jnp.ones((PACK, rows), BF16), step[:, here])
            keep = jnp.concatenate([keep_all] * len(tiles), axis=1)
            through = jnp.exp2(rate_of(here) * total[0:1, :]) * keep
            outbox[chunk] = through * inbox[chunk] + ends[chunk]
            relay_copy(chunk).start()

    after = seq_total - 1 - seq
    is_first = lax.div(after, seq_total - 1)
    is_far = lax.div(lax.div(after, chunks) + seq_total - 1, seq_total)
    late = is_first + is_far - is_first * is_far
    lag = late * chunks + (1 - late) * after

    def scan_chunk(chunk, _):
        here = pl.ds(pl.multiple_of(chunk * CHUNK, CHUNK), CHUNK)
        grad_f[...] = grad[:, here].astype(F32)
        for t, at in zip(tiles, chunk_tiles(chunk)):
            step_f[:, t] = step[:, at].astype(F32) + reset[...]
        rates = [rate_of(at) for at in chunk_tiles(chunk)]

        def one_group(index, carry):
            group = rows // GROUP - 1 - index
            first = pl.multiple_of(group * GROUP, GROUP)
            near_step = step_f.at[pl.ds(first, GROUP), :]
            near_grad = grad_f.at[pl.ds(first, GROUP), :]
            for pair in reversed(range(GROUP // 2)):
                sums = [None, None]
                for which in (1, 0):
                    offset = 2 * pair + which
                    at = pl.ds(pl.multiple_of((first + offset) * count, count), count)
                    weight, reader = out_table[at, :], in_table[at, :]
                    one = slice(offset, offset + 1)
                    fresh, sums[which] = [], []
                    for t, a, held in zip(tiles, rates, carry):
                        adjoint = weight * near_grad[one, t] + held
                        sums[which].append(folded(reader * adjoint))
                        fresh.append(jnp.exp2(near_step[one, t] * a) * adjoint)
                    carry = fresh
                for t, low, high in zip(tiles, *sums):
                    both = jnp.concatenate([low, high], axis=0)
                    states[pair * PACK : (pair + 1) * PACK, t] = both.astype(BF16)
            local_y[pl.ds(first, GROUP), here] = dot(in_diag[pl.ds(first, GROUP), :], states[...])
            return carry

        start = [jnp.zeros((count, LANES), F32) for _ in tiles]
        last = lax.fori_loop(0, rows // GROUP, one_group, start)
        for t, value in zip(tiles, last):
            ends[chunk, :, t] = value

        @pl.when(chunk >= lag)
        def _():
            relay(chunk - lag)

        return 0

    lax.fori_loop(0, chunks, scan_chunk, 0)
    out_own[...] = jnp.zeros_like(out_own)
    later = (
        lax.broadcasted_iota(jnp.int32, (rows, rows), 0)
        < lax.broadcasted_iota(jnp.int32, (rows, rows), 1)
    ).astype(F32).astype(BF16)

    def join_chunk(chunk, _):
        @pl.when(chunk < lag)
        def _():
            relay(chunks + chunk - lag)

        here = pl.ds(pl.multiple_of(chunk * CHUNK, CHUNK), CHUNK)
        step_f[...] = dot(later, step[:, here])
        rates = [rate_of(at) for at in chunk_tiles(chunk)]
        enters = [inbox[chunk, :, t] for t in tiles]

        def one_group(group, _):
            first = pl.multiple_of(group * GROUP, GROUP)
            near = step_f.at[pl.ds(first, GROUP), :]
            for pair in range(GROUP // 2):
                readers = []
                for offset in (2 * pair, 2 * pair + 1):
                    at = pl.ds(pl.multiple_of((first + offset) * count, count), count)
                    readers.append((slice(offset, offset + 1), in_table[at, :]))
                for t, a, e in zip(tiles, rates, enters):
                    both = jnp.concatenate(
                        [folded(jnp.exp2(near[one, t] * a) * e * b) for one, b in readers], axis=0
                    )
                    states[pair * PACK : (pair + 1) * PACK, t] = both.astype(BF16)
            lines = pl.ds(first, GROUP)
            total = local_y[lines, here] + dot(open_diag[lines, :], states[...])
            result = skip[:, here] * grad[lines, here].astype(F32) + step[lines, here].astype(
                F32
            ) * total
            mixed[lines, :] = result.astype(BF16)
            return 0

        lax.fori_loop(0, rows // GROUP, one_group, 0)
        out_own[...] += dot(out_sketch[:, here], mixed[...], LAST)
        return 0

    lax.fori_loop(0, chunks, join_chunk, 0)

    pair_copy(out_own, out_peer, 1).start()
    pair_copy(in_own, in_peer, 0).wait()
    in_side = (in_own[...] + in_peer[...]).astype(BF16)
    pair_copy(out_own, out_peer, 1).wait()
    out_side = (out_own[...] + out_peer[...]).astype(BF16)

    def one_owner(owner, _):
        sketch_part[owner] = dot(out_side, in_side * member[owner])
        return 0

    lax.fori_loop(0, seq_total, one_owner, 0)
    for offset in range(1, seq_total):
        sketch_copy(offset).start()

    @pl.when(seq > 0)
    def _():
        for chunk in range(chunks):
            relay_copy(chunk).wait_send()

    for offset in range(1, team):
        query_copy(offset).wait()
    query_all[quarter] = queries[...]
    total = sketch_part[seq]
    for offset in range(1, seq_total):
        sketch_copy(offset).wait()
        total += sketch_peer[offset - 1]

    entry = lax.broadcasted_iota(jnp.int32, (LANES, LANES), 0) // side
    same = (entry == lax.broadcasted_iota(jnp.int32, (LANES, LANES), 1) // side).astype(F32)
    squares = jnp.broadcast_to(jnp.sum(total * total, axis=0, keepdims=True), (8, LANES))
    mean_square = dot(squares, same, precision=lax.Precision.HIGHEST)[0:1] / (side * side)
    normed = (total * lax.rsqrt(mean_square + EPSILON)).astype(BF16).astype(F32)
    half = (
        lax.broadcasted_iota(jnp.int32, (8, LANES), 0)
        == lax.broadcasted_iota(jnp.int32, (8, LANES), 1) // side
    ).astype(F32)
    local_queries = queries.shape[0]
    for index in range(team):
        product = query_all[index].astype(F32) * normed[None]
        columns = jnp.sum(product, axis=1)
        value = dot(half, columns, LAST, precision=lax.Precision.HIGHEST)
        scores[:, index * local_queries : (index + 1) * local_queries] = value[:owned]


def local(
    hidden_rows,
    scan_grad,
    step_size,
    state_proj,
    decay_rate,
    skip_gain,
    in_sketch,
    out_sketch,
    doc_lengths,
    doc_slot,
    query_sketch,
):
    seq_total = lax.axis_size("seq")
    query_total = lax.axis_size("query")
    chan_total = lax.axis_size("chan")
    rows, channels = scan_grad.shape[1:]
    count = decay_rate.shape[0]
    docs = doc_lengths.shape[1]
    side = in_sketch.shape[1]
    owned = docs // seq_total
    chunks = channels // CHUNK
    team = query_total * chan_total
    local_queries = query_sketch.shape[0]
    square = query_sketch.reshape(local_queries, side, side)
    queries = jnp.concatenate([square] * owned, axis=2)
    in_wide = jnp.concatenate([in_sketch.T] * owned, axis=0)
    vmem = pl.BlockSpec(memory_space=pltpu.VMEM)
    smem = pl.BlockSpec(memory_space=pltpu.SMEM)
    dma = pltpu.SemaphoreType.DMA
    scores = pl.pallas_call(
        functools.partial(kernel, seq_total, query_total, chan_total),
        in_specs=[smem, smem] + [vmem] * 9,
        out_specs=vmem,
        out_shape=jax.ShapeDtypeStruct((owned, team * local_queries), F32),
        scratch_shapes=[
            pltpu.VMEM((rows, CHUNK), F32),
            pltpu.VMEM((rows, CHUNK), F32),
            pltpu.VMEM((GROUP * FOLD, CHUNK), BF16),
            pltpu.VMEM((rows, channels), F32),
            pltpu.VMEM((rows, CHUNK), BF16),
            pltpu.VMEM((rows * count, LANES), F32),
            pltpu.VMEM((rows * count, LANES), F32),
            pltpu.VMEM((rows, GROUP * FOLD), BF16),
            pltpu.VMEM((rows, GROUP * FOLD), BF16),
            pltpu.VMEM((rows, LANES), F32),
            pltpu.VMEM((seq_total, rows, LANES), BF16),
            pltpu.VMEM((chunks, count, CHUNK), F32),
            pltpu.VMEM((chunks, count, CHUNK), F32),
            pltpu.VMEM((chunks, count, CHUNK), F32),
            pltpu.VMEM((rows, LANES), F32),
            pltpu.VMEM((rows, LANES), F32),
            pltpu.VMEM((side, rows), F32),
            pltpu.VMEM((side, rows), F32),
            pltpu.VMEM((seq_total, side, LANES), F32),
            pltpu.VMEM((seq_total - 1, side, LANES), F32),
            pltpu.VMEM((team, local_queries, side, LANES), BF16),
            dma((chunks,)),
            dma((chunks,)),
            dma((2,)),
            dma((2,)),
            dma((team - 1,)),
            dma((team - 1,)),
            dma((seq_total - 1,)),
            dma((seq_total - 1,)),
        ],
        compiler_params=pltpu.CompilerParams(
            vmem_limit_bytes=52 * 2**20, collective_id=0, has_side_effects=True
        ),
        name="sketch_scores",
    )(
        doc_lengths,
        doc_slot,
        hidden_rows[0],
        scan_grad[0],
        step_size[0],
        state_proj[0],
        decay_rate,
        skip_gain[None, :],
        in_wide,
        out_sketch.T,
        queries,
    )
    return scores[None]


def solution(mesh):
    placed = (
        P(("groups", "query"), "seq", "chan"),
        P(("groups", "query"), "seq", "chan"),
        P(("groups", "query"), "seq", "chan"),
        P(("groups", "query"), None, None, "seq"),
        P(None, "chan"),
        P("chan"),
        P("chan", None),
        P("chan", None),
        P(("groups", "query"), None),
        P(("groups", "query"), None),
        P(("query", "chan"), None),
    )
    return jax.shard_map(
        local,
        mesh=mesh,
        in_specs=placed,
        out_specs=P(("groups", "query"), "seq", None),
        check_vma=False,
    )
```

```python
import functools
import math

import jax
import jax.numpy as jnp
from jax import lax
from jax.experimental import pallas as pl
from jax.experimental.pallas import tpu as pltpu
from jax.sharding import PartitionSpec as P

EPSILON = 1e-06
LANES = 128
GROUP = 32
FOLD = 8
PACK = 16
CHUNK = 1024
TINY = 1.1754944e-38
F32 = jnp.float32
BF16 = jnp.bfloat16
MESH = pl.DeviceIdType.MESH
LAST = (((1,), (1,)), ((), ()))
FIRST = (((0,), (0,)), ((), ()))


def lane_tiles(width):
    return [slice(t * LANES, (t + 1) * LANES) for t in range(width // LANES)]


def dot(a, b, dims=None, precision=None):
    if dims is None:
        dims = (((1,), (0,)), ((), ()))
    return lax.dot_general(a, b, dims, preferred_element_type=F32, precision=precision)


def kernel(
    seq_total,
    query_total,
    chan_total,
    lengths_in,
    slots_in,
    hidden_in,
    grad_in,
    step_in,
    proj_in,
    decay_in,
    skip_in,
    in_sketch,
    out_sketch_in,
    queries,
    scores,
    lengths,
    slots,
    hidden,
    grad,
    step,
    proj,
    decay,
    skip,
    out_sketch,
    step_f,
    grad_f,
    states,
    local_y,
    mixed,
    out_table,
    in_table,
    in_diag,
    open_diag,
    reset,
    member,
    ends,
    inbox,
    outbox,
    in_own,
    in_peer,
    out_own,
    out_peer,
    sketch_part,
    sketch_peer,
    query_all,
    relay_send,
    relay_recv,
    pair_send,
    pair_recv,
    query_send,
    query_recv,
    sketch_send,
    sketch_recv,
    load_sems,
):
    rows, channels = grad.shape
    count = decay.shape[0]
    docs = lengths.shape[1]
    owned = docs // seq_total
    side = LANES // owned
    chunks = channels // CHUNK
    tiles = lane_tiles(CHUNK)
    seq = lax.axis_index("seq")
    query = lax.axis_index("query")
    chan = lax.axis_index("chan")
    quarter = query * chan_total + chan
    team = query_total * chan_total

    def seq_peer(offset):
        return {"seq": lax.rem(seq + offset, seq_total)}

    def team_peer(offset):
        other = lax.rem(quarter + offset, team)
        return {"query": lax.div(other, chan_total), "chan": lax.rem(other, chan_total)}

    loads = [
        pltpu.make_async_copy(source, target, load_sems.at[i])
        for i, (source, target) in enumerate(
            (
                (lengths_in, lengths),
                (slots_in, slots),
                (proj_in, proj),
                (hidden_in, hidden),
                (decay_in, decay),
                (step_in, step),
                (grad_in, grad),
                (skip_in, skip),
                (out_sketch_in, out_sketch),
            )
        )
    ]
    for load in loads:
        load.start()

    barrier = pltpu.get_barrier_semaphore()
    for offset in range(1, seq_total):
        pl.semaphore_signal(barrier, inc=1, device_id=seq_peer(offset), device_id_type=MESH)
    for offset in range(1, team):
        pl.semaphore_signal(barrier, inc=1, device_id=team_peer(offset), device_id_type=MESH)
    pl.semaphore_wait(barrier, seq_total + team - 2)

    def query_copy(offset):
        return pltpu.make_async_remote_copy(
            src_ref=queries,
            dst_ref=query_all.at[quarter],
            send_sem=query_send.at[offset - 1],
            recv_sem=query_recv.at[offset - 1],
            device_id=team_peer(offset),
            device_id_type=MESH,
        )

    def pair_copy(source, target, index):
        return pltpu.make_async_remote_copy(
            src_ref=source,
            dst_ref=target,
            send_sem=pair_send.at[index],
            recv_sem=pair_recv.at[index],
            device_id={"chan": 1 - chan},
            device_id_type=MESH,
        )

    def relay_copy(index):
        return pltpu.make_async_remote_copy(
            src_ref=outbox.at[index],
            dst_ref=inbox.at[index],
            send_sem=relay_send.at[index],
            recv_sem=relay_recv.at[index],
            device_id={"seq": lax.rem(seq + seq_total - 1, seq_total)},
            device_id_type=MESH,
        )

    def sketch_copy(offset):
        return pltpu.make_async_remote_copy(
            src_ref=sketch_part.at[lax.rem(seq + offset, seq_total)],
            dst_ref=sketch_peer.at[offset - 1],
            send_sem=sketch_send.at[offset - 1],
            recv_sem=sketch_recv.at[offset - 1],
            device_id=seq_peer(offset),
            device_id_type=MESH,
        )

    for offset in range(1, team):
        query_copy(offset).start()

    for load in loads[:3]:
        load.wait()
    begin = seq * rows
    line = begin + lax.broadcasted_iota(jnp.int32, (rows, LANES), 0)
    lane_slot = lax.broadcasted_iota(jnp.int32, (rows, LANES), 1) // side

    def mark_starts(k, carry):
        start, is_start, is_shut, is_any = carry
        is_start = jnp.where(line == start, 1.0, is_start)
        inside = (start > line) & (start < begin + rows)
        is_shut = jnp.where(inside, 1.0, is_shut)
        first = jnp.full(is_any.shape, start, jnp.int32)
        held = (first >= begin) & (first < begin + rows)
        is_any = jnp.where(held, 1.0, is_any)
        return start + lengths[0, k], is_start, is_shut, is_any

    empty = jnp.zeros((rows, LANES), F32)
    _, is_start, is_shut, is_any = lax.fori_loop(
        0, docs, mark_starts, (jnp.int32(0), empty, empty, jnp.zeros((count, LANES), F32))
    )
    reset[...] = jnp.where(is_start > 0.0, jnp.inf, 0.0)
    keep_all = 1.0 - is_any
    is_open = 1.0 - is_shut

    def owner_mask(owner, _):
        def mark(k, carry):
            start, mask = carry
            stop = start + lengths[0, k]
            hit = (lane_slot + owner * owned == slots[0, k]) & (line >= start) & (line < stop)
            return stop, jnp.where(hit, 1.0, mask)

        _, mask = lax.fori_loop(0, docs, mark, (jnp.int32(0), empty))
        member[owner] = mask.astype(BF16)
        return 0

    lax.fori_loop(0, seq_total, owner_mask, 0)

    wide = (PACK * count, rows)
    row_place = lax.broadcasted_iota(jnp.int32, wide, 0) // count
    row_line = lax.broadcasted_iota(jnp.int32, wide, 1)
    ones = jnp.ones((rows, LANES), BF16)
    spreads = [jnp.concatenate([proj[i].astype(F32)] * PACK, axis=0) for i in range(2)]

    def fill_tables(group, _):
        here = pl.ds(pl.multiple_of(group * PACK * count, PACK * count), PACK * count)
        for table, spread in zip((in_table, out_table), spreads):
            picked = jnp.where(row_line == row_place + group * PACK, spread, 0.0).astype(BF16)
            table[here, :] = dot(picked, ones)
        return 0

    lax.fori_loop(0, rows // PACK, fill_tables, 0)

    deep = (rows, GROUP * FOLD)
    on_line = lax.rem(lax.broadcasted_iota(jnp.int32, deep, 0), GROUP) == (
        lax.broadcasted_iota(jnp.int32, deep, 1) // FOLD
    )
    diag = on_line.astype(F32)
    in_diag[...] = diag.astype(BF16)
    open_wide = jnp.concatenate([is_open] * (GROUP * FOLD // LANES), axis=1)
    open_diag[...] = (diag * open_wide).astype(BF16)

    def folded(value):
        parts = [value[i : i + FOLD] for i in range(0, count, FOLD)]
        return sum(parts[1:], parts[0])

    loads[3].wait()
    in_own[...] = dot(hidden[...], in_sketch[...], LAST)
    pair_copy(in_own, in_peer, 0).start()
    for load in loads[4:]:
        load.wait()

    def rate_of(columns):
        return -jnp.maximum(decay[:, columns] * math.log2(math.e), TINY)

    def chunk_tiles(chunk):
        base = chunk * CHUNK
        return [pl.ds(pl.multiple_of(base + t * LANES, LANES), LANES) for t in range(len(tiles))]

    def relay(chunk):
        @pl.when(seq < seq_total - 1)
        def _():
            relay_copy(chunk).wait_recv()

        @pl.when(seq == seq_total - 1)
        def _():
            inbox[chunk] = jnp.zeros((count, CHUNK), F32)

        @pl.when(seq > 0)
        def _():
            here = pl.ds(pl.multiple_of(chunk * CHUNK, CHUNK), CHUNK)
            total = dot(jnp.ones((PACK, rows), BF16), step[:, here])
            keep = jnp.concatenate([keep_all] * len(tiles), axis=1)
            through = jnp.exp2(rate_of(here) * total[0:1, :]) * keep
            outbox[chunk] = through * inbox[chunk] + ends[chunk]
            relay_copy(chunk).start()

    after = seq_total - 1 - seq
    is_first = lax.div(after, seq_total - 1)
    is_far = lax.div(lax.div(after, chunks) + seq_total - 1, seq_total)
    late = is_first + is_far - is_first * is_far
    lag = late * chunks + (1 - late) * after

    def scan_chunk(chunk, _):
        here = pl.ds(pl.multiple_of(chunk * CHUNK, CHUNK), CHUNK)
        grad_f[...] = grad[:, here].astype(F32)
        for t, at in zip(tiles, chunk_tiles(chunk)):
            step_f[:, t] = step[:, at].astype(F32) + reset[...]
        rates = [rate_of(at) for at in chunk_tiles(chunk)]

        def one_group(index, carry):
            group = rows // GROUP - 1 - index
            first = pl.multiple_of(group * GROUP, GROUP)
            near_step = step_f.at[pl.ds(first, GROUP), :]
            near_grad = grad_f.at[pl.ds(first, GROUP), :]
            for pair in reversed(range(GROUP // 2)):
                sums = [None, None]
                for which in (1, 0):
                    offset = 2 * pair + which
                    at = pl.ds(pl.multiple_of((first + offset) * count, count), count)
                    weight, reader = out_table[at, :], in_table[at, :]
                    one = slice(offset, offset + 1)
                    fresh, sums[which] = [], []
                    for t, a, held in zip(tiles, rates, carry):
                        adjoint = weight * near_grad[one, t] + held
                        sums[which].append(folded(reader * adjoint))
                        fresh.append(jnp.exp2(near_step[one, t] * a) * adjoint)
                    carry = fresh
                for t, low, high in zip(tiles, *sums):
                    both = jnp.concatenate([low, high], axis=0)
                    states[pair * PACK : (pair + 1) * PACK, t] = both.astype(BF16)
            local_y[pl.ds(first, GROUP), here] = dot(in_diag[pl.ds(first, GROUP), :], states[...])
            return carry

        start = [jnp.zeros((count, LANES), F32) for _ in tiles]
        last = lax.fori_loop(0, rows // GROUP, one_group, start)
        for t, value in zip(tiles, last):
            ends[chunk, :, t] = value

        @pl.when(chunk >= lag)
        def _():
            relay(chunk - lag)

        return 0

    lax.fori_loop(0, chunks, scan_chunk, 0)
    out_own[...] = jnp.zeros_like(out_own)
    later = (
        lax.broadcasted_iota(jnp.int32, (rows, rows), 0)
        < lax.broadcasted_iota(jnp.int32, (rows, rows), 1)
    ).astype(F32).astype(BF16)

    def join_chunk(chunk, _):
        @pl.when(chunk < lag)
        def _():
            relay(chunks + chunk - lag)

        here = pl.ds(pl.multiple_of(chunk * CHUNK, CHUNK), CHUNK)
        step_f[...] = dot(later, step[:, here])
        rates = [rate_of(at) for at in chunk_tiles(chunk)]
        enters = [inbox[chunk, :, t] for t in tiles]

        def one_group(group, _):
            first = pl.multiple_of(group * GROUP, GROUP)
            near = step_f.at[pl.ds(first, GROUP), :]
            for pair in range(GROUP // 2):
                readers = []
                for offset in (2 * pair, 2 * pair + 1):
                    at = pl.ds(pl.multiple_of((first + offset) * count, count), count)
                    readers.append((slice(offset, offset + 1), in_table[at, :]))
                for t, a, e in zip(tiles, rates, enters):
                    both = jnp.concatenate(
                        [folded(jnp.exp2(near[one, t] * a) * e * b) for one, b in readers], axis=0
                    )
                    states[pair * PACK : (pair + 1) * PACK, t] = both.astype(BF16)
            lines = pl.ds(first, GROUP)
            total = local_y[lines, here] + dot(open_diag[lines, :], states[...])
            result = skip[:, here] * grad[lines, here].astype(F32) + step[lines, here].astype(
                F32
            ) * total
            mixed[lines, :] = result.astype(BF16)
            return 0

        lax.fori_loop(0, rows // GROUP, one_group, 0)
        out_own[...] += dot(out_sketch[:, here], mixed[...], LAST)
        return 0

    lax.fori_loop(0, chunks, join_chunk, 0)

    pair_copy(out_own, out_peer, 1).start()
    pair_copy(in_own, in_peer, 0).wait()
    in_side = (in_own[...] + in_peer[...]).astype(BF16)
    pair_copy(out_own, out_peer, 1).wait()
    out_side = (out_own[...] + out_peer[...]).astype(BF16)

    def one_owner(owner, _):
        sketch_part[owner] = dot(out_side, in_side * member[owner])
        return 0

    lax.fori_loop(0, seq_total, one_owner, 0)
    for offset in range(1, seq_total):
        sketch_copy(offset).start()

    @pl.when(seq > 0)
    def _():
        for chunk in range(chunks):
            relay_copy(chunk).wait_send()

    for offset in range(1, team):
        query_copy(offset).wait()
    query_all[quarter] = queries[...]
    total = sketch_part[seq]
    for offset in range(1, seq_total):
        sketch_copy(offset).wait()
        total += sketch_peer[offset - 1]

    entry = lax.broadcasted_iota(jnp.int32, (LANES, LANES), 0) // side
    same = (entry == lax.broadcasted_iota(jnp.int32, (LANES, LANES), 1) // side).astype(F32)
    squares = jnp.broadcast_to(jnp.sum(total * total, axis=0, keepdims=True), (8, LANES))
    mean_square = dot(squares, same, precision=lax.Precision.HIGHEST)[0:1] / (side * side)
    normed = (total * lax.rsqrt(mean_square + EPSILON)).astype(BF16).astype(F32)
    half = (
        lax.broadcasted_iota(jnp.int32, (8, LANES), 0)
        == lax.broadcasted_iota(jnp.int32, (8, LANES), 1) // side
    ).astype(F32)
    local_queries = queries.shape[0]
    for index in range(team):
        product = query_all[index].astype(F32) * normed[None]
        columns = jnp.sum(product, axis=1)
        value = dot(half, columns, LAST, precision=lax.Precision.HIGHEST)
        scores[:, index * local_queries : (index + 1) * local_queries] = value[:owned]


def local(
    hidden_rows,
    scan_grad,
    step_size,
    state_proj,
    decay_rate,
    skip_gain,
    in_sketch,
    out_sketch,
    doc_lengths,
    doc_slot,
    query_sketch,
):
    seq_total = lax.axis_size("seq")
    query_total = lax.axis_size("query")
    chan_total = lax.axis_size("chan")
    rows, channels = scan_grad.shape[1:]
    count = decay_rate.shape[0]
    docs = doc_lengths.shape[1]
    side = in_sketch.shape[1]
    owned = docs // seq_total
    chunks = channels // CHUNK
    team = query_total * chan_total
    local_queries = query_sketch.shape[0]
    square = query_sketch.reshape(local_queries, side, side)
    queries = jnp.concatenate([square] * owned, axis=2)
    in_wide = jnp.concatenate([in_sketch.T] * owned, axis=0)
    vmem = pl.BlockSpec(memory_space=pltpu.VMEM)
    anywhere = pl.BlockSpec(memory_space=pltpu.HBM)
    dma = pltpu.SemaphoreType.DMA
    scores = pl.pallas_call(
        functools.partial(kernel, seq_total, query_total, chan_total),
        in_specs=[anywhere] * 8 + [vmem, anywhere, vmem],
        out_specs=vmem,
        out_shape=jax.ShapeDtypeStruct((owned, team * local_queries), F32),
        scratch_shapes=[
            pltpu.SMEM((1, docs), jnp.int32),
            pltpu.SMEM((1, docs), jnp.int32),
            pltpu.VMEM(hidden_rows.shape[1:], BF16),
            pltpu.VMEM((rows, channels), BF16),
            pltpu.VMEM((rows, channels), BF16),
            pltpu.VMEM(state_proj.shape[1:], BF16),
            pltpu.VMEM(decay_rate.shape, F32),
            pltpu.VMEM((1, channels), F32),
            pltpu.VMEM((side, channels), BF16),
            pltpu.VMEM((rows, CHUNK), F32),
            pltpu.VMEM((rows, CHUNK), F32),
            pltpu.VMEM((GROUP * FOLD, CHUNK), BF16),
            pltpu.VMEM((rows, channels), F32),
            pltpu.VMEM((rows, CHUNK), BF16),
            pltpu.VMEM((rows * count, LANES), F32),
            pltpu.VMEM((rows * count, LANES), F32),
            pltpu.VMEM((rows, GROUP * FOLD), BF16),
            pltpu.VMEM((rows, GROUP * FOLD), BF16),
            pltpu.VMEM((rows, LANES), F32),
            pltpu.VMEM((seq_total, rows, LANES), BF16),
            pltpu.VMEM((chunks, count, CHUNK), F32),
            pltpu.VMEM((chunks, count, CHUNK), F32),
            pltpu.VMEM((chunks, count, CHUNK), F32),
            pltpu.VMEM((rows, LANES), F32),
            pltpu.VMEM((rows, LANES), F32),
            pltpu.VMEM((side, rows), F32),
            pltpu.VMEM((side, rows), F32),
            pltpu.VMEM((seq_total, side, LANES), F32),
            pltpu.VMEM((seq_total - 1, side, LANES), F32),
            pltpu.VMEM((team, local_queries, side, LANES), BF16),
            dma((chunks,)),
            dma((chunks,)),
            dma((2,)),
            dma((2,)),
            dma((team - 1,)),
            dma((team - 1,)),
            dma((seq_total - 1,)),
            dma((seq_total - 1,)),
            dma((9,)),
        ],
        compiler_params=pltpu.CompilerParams(
            vmem_limit_bytes=64 * 2**20, collective_id=0, has_side_effects=True
        ),
        name="sketch_scores",
    )(
        doc_lengths,
        doc_slot,
        hidden_rows[0],
        scan_grad[0],
        step_size[0],
        state_proj[0],
        decay_rate,
        skip_gain[None, :],
        in_wide,
        out_sketch.T,
        queries,
    )
    return scores[None]


def solution(mesh):
    placed = (
        P(("groups", "query"), "seq", "chan"),
        P(("groups", "query"), "seq", "chan"),
        P(("groups", "query"), "seq", "chan"),
        P(("groups", "query"), None, None, "seq"),
        P(None, "chan"),
        P("chan"),
        P("chan", None),
        P("chan", None),
        P(("groups", "query"), None),
        P(("groups", "query"), None),
        P(("query", "chan"), None),
    )
    return jax.shard_map(
        local,
        mesh=mesh,
        in_specs=placed,
        out_specs=P(("groups", "query"), "seq", None),
        check_vma=False,
    )
```
